32 devices in a mesh: ex: 8 (over y, x, core), ey: 4 (over z).
Axes of the slice: x: 2, y: 2, z: 4, core: 2. Of those that a mesh axis runs over, the one named last changes fastest.
Arguments:
- settings: float32 [512, 16], replicated, may hold values from -1 to 1
- frequencies: float32 [16, 2048], replicated, may hold values from -4 to 4
- phases: float32 [2048], replicated, may hold values from -3.140625 to 3.140625
- noise_var: float32 [128], replicated, may hold values from 0.01 to 0.1
- signal_scale: float32 [128], replicated, may hold values from 0.5 to 2
- cov_factor: bfloat16 [64, 2048, 2048], P(('ex', 'ey')), as said below
- post_mean: bfloat16 [64, 2048, 128], P(('ex', 'ey')), may hold values from -6 to 6
- component_basis: bfloat16 [128, 262144], P('ey', 'ex'), may hold values from -0.5 to 0.5
- mean_field: float32 [262144], P(('ex', 'ey')), may hold values from -4 to 4
Outputs:
- carbon: bfloat16 [512, 262144], P(None, ('ex', 'ey'))
The draws below stay inside these ranges and needn't reach their ends.
Inputs may be any that keep to these rules, and one draw needn't show every extreme that they name: `cov_factor`: entries of expert k's factor lie within 8 / sqrt(log(2049)) of zero.
All inputs are finite; a program needn't handle non-finite values.
Results may differ from the reference program's by a relative error of at most 0.0037.
Values may be sent and summed in bfloat16 or wider, within the bound.
A program may use at most 128 MiB of HBM per device.

```python
import math
import jax
import jax.numpy as jnp
from jax import lax

PARAMS = 16
FEAT = 2048
COMP = 128
SETTINGS = 512
EXPERTS = 64
CELLS = 262144


def draw_cov_factor(key, part):
    key_gain = jax.random.fold_in(key, 11)
    key_noise = jax.random.fold_in(key, 23)
    key_column = jax.random.fold_in(key, 37)
    gains = jnp.exp(jax.random.uniform(key_gain, (EXPERTS, 1, 1), jnp.float32, math.log(0.2), math.log(2.0)))
    draws_column = jax.random.uniform(key_column, (EXPERTS, 1, FEAT), jnp.float32, 0.0, 1.0)
    column_weight = 1.0 / (1.0 + draws_column * FEAT)
    column_scale = jnp.sqrt(column_weight / math.log(1.0 + FEAT))
    values = jax.random.truncated_normal(key_noise, -4.0, 4.0, (EXPERTS, FEAT, FEAT), jnp.float32)
    return (values * gains * column_scale).astype(jnp.bfloat16)


def level_of(stream_key, extent, cuts, least, top_value):
    loudness, own = 1.0, jax.random.fold_in(stream_key, 6)
    for dim, parts in cuts:
        draws = jnp.exp(jax.random.uniform(jax.random.fold_in(own, dim), (parts,), jnp.float32, least / len(cuts), top_value / len(cuts)))
        loudness = loudness * jnp.repeat(draws, extent[dim] // parts).reshape([-1 if axis == dim else 1 for axis in range(len(extent))])
    return loudness


def gaussian(own_key, dims, width, most, cuts=(), dtype=jnp.bfloat16):
    array = width * jax.random.normal(own_key, dims, jnp.float32)
    if cuts:
        array = array * level_of(own_key, dims, cuts, -0.22, 0.18)
    return jnp.clip(array, -most, most).astype(dtype)


def setup_inputs(seed: int = 0) -> dict:
    arg_keys = jax.random.split(jax.random.key(seed), 10)
    settings = jnp.clip(jax.random.uniform(arg_keys[0], (SETTINGS, PARAMS), jnp.float32, -1.0, 1.0), -1.0, 1.0)
    frequencies = gaussian(arg_keys[1], (PARAMS, FEAT), 1.0, 4.0, (), jnp.float32)
    phases = jnp.clip(jax.random.uniform(arg_keys[2], (FEAT,), jnp.float32, -3.140625, 3.140625), -3.140625, 3.140625)
    noise_var = jnp.clip(jnp.exp(jax.random.uniform(arg_keys[3], (COMP,), jnp.float32, math.log(0.01), math.log(0.1))), 0.01, 0.1)
    signal_scale = jnp.clip(jnp.exp(jax.random.uniform(arg_keys[4], (COMP,), jnp.float32, math.log(0.5), math.log(2.0))), 0.5, 2.0)
    cov_factor = draw_cov_factor(jax.random.fold_in(arg_keys[9], 71), 0)
    post_mean = gaussian(arg_keys[6], (EXPERTS, FEAT, COMP), 1.0, 6.0, ((0, 32),))
    component_basis = gaussian(arg_keys[7], (COMP, CELLS), COMP ** -0.5, 0.5, ((0, 4), (1, 8)))
    mean_field = gaussian(arg_keys[8], (CELLS,), 0.25, 4.0, ((0, 32),), jnp.float32)
    return {"settings": settings, "frequencies": frequencies, "phases": phases, "noise_var": noise_var, "signal_scale": signal_scale, "cov_factor": cov_factor, "post_mean": post_mean, "component_basis": component_basis, "mean_field": mean_field}


def feature_map(settings, frequencies, phases):
    argument = jnp.dot(settings, frequencies, precision=lax.Precision.HIGHEST, preferred_element_type=jnp.float32)
    return (jnp.sqrt(2.0 / FEAT) * jnp.cos(argument + phases[None, :])).astype(jnp.bfloat16)

def reference(settings, frequencies, phases, noise_var, signal_scale, cov_factor, post_mean, component_basis, mean_field):
    feature_rows = feature_map(settings, frequencies, phases)
    feature_float = feature_rows.astype(jnp.float32)
    feature_norm = lax.optimization_barrier(jnp.sum(feature_float * feature_float, axis=1))
    prior_var = noise_var[None, :] + signal_scale[None, :] * feature_norm[:, None]

    def accumulate(running, operands):
        numerator, precision = running
        factor, expert_means = operands
        projected = jnp.dot(feature_rows, factor, preferred_element_type=jnp.float32)
        spread = lax.optimization_barrier(jnp.sum(projected * projected, axis=1))
        expert_mean = jnp.dot(feature_rows, expert_means, preferred_element_type=jnp.float32)
        variance = noise_var[None, :] + signal_scale[None, :] * spread[:, None]
        robust_weight = jnp.maximum(0.5 * (jnp.log(prior_var) - jnp.log(variance)), 0.0)
        numerator = numerator + robust_weight / variance * expert_mean
        precision = precision + robust_weight * (1.0 / variance - 1.0 / prior_var)
        return ((numerator, precision), None)
    zeros_init = jnp.zeros((SETTINGS, COMP), jnp.float32)
    (numerator, precision), _ = lax.scan(accumulate, (zeros_init, zeros_init), (cov_factor, post_mean))
    weights = (numerator / (precision + 1.0 / prior_var)).astype(jnp.bfloat16)
    stock = jnp.dot(weights, component_basis, preferred_element_type=jnp.float32) + mean_field[None, :]
    return stock.astype(jnp.bfloat16)
```

```python
import functools
import math

import jax
import jax.numpy as jnp
from jax import lax
from jax.experimental import pallas as pl
from jax.experimental.pallas import tpu as pltpu
from jax.sharding import PartitionSpec as P

CHUNKS = 4
TILE = 512
FEAT_TILE = 256
COS_POLY = (0.9999999532, -4.9347928306, 4.0584113529, -1.3318765681, 0.2196896111)


def split3(x):
    first = x.astype(jnp.bfloat16)
    rest = x - first.astype(jnp.float32)
    second = rest.astype(jnp.bfloat16)
    third = (rest - second.astype(jnp.float32)).astype(jnp.bfloat16)
    return first, second, third


def experts_kernel(
    nx, ny,
    settings, frequencies, phases, noise_var, signal_scale, cov, post, basis,
    relaid, weights,
    phi, freq_stack, cov_buf, post_buf, norm_acc, spread_acc, inv_prior,
    parts, plane_in, column_out, column_in, gathered,
    cov_sem, post_sem, own_sem,
    basis_send, basis_recv, plane_send, plane_recv,
    column_send, column_recv, gather_send, gather_recv,
):
    ex = lax.axis_index("ex")
    ey = lax.axis_index("ey")
    n_exp, feat, _ = cov.shape
    n_set = settings.shape[0]
    n_par = settings.shape[1]
    comp = noise_var.shape[1]
    rows = basis.shape[0]
    cells = basis.shape[1] // ny
    chunk = cells // CHUNKS
    block = n_set // nx
    tiles = feat // TILE

    barrier = pltpu.get_barrier_semaphore()
    for d in range(1, ny):
        pl.semaphore_signal(barrier, inc=1, device_id={"ey": lax.rem(ey + d, ny)})
    for d in range(1, nx):
        pl.semaphore_signal(barrier, inc=1, device_id={"ex": lax.rem(ex + d, nx)})

    def cov_copy(i):
        e = i // tiles
        cols = pl.ds(pl.multiple_of((i % tiles) * TILE, TILE), TILE)
        return pltpu.make_async_copy(cov.at[e, :, cols], cov_buf.at[i], cov_sem.at[i])

    def post_copy(e):
        return pltpu.make_async_copy(
            post.at[e], post_buf.at[:, pl.ds(e * comp, comp)], post_sem.at[e]
        )

    for i in range(n_exp * tiles):
        cov_copy(i).start()
    for e in range(n_exp):
        post_copy(e).start()

    pl.semaphore_wait(barrier, (nx - 1) + (ny - 1))

    def basis_copy(d, c):
        to = lax.rem(ey + d, ny)
        k = (d - 1) * CHUNKS + c
        return pltpu.make_async_remote_copy(
            src_ref=basis.at[:, pl.ds(pl.multiple_of(to * cells + c * chunk, 128), chunk)],
            dst_ref=relaid.at[pl.ds(pl.multiple_of(ey * rows, rows), rows), pl.ds(c * chunk, chunk)],
            send_sem=basis_send.at[k],
            recv_sem=basis_recv.at[k],
            device_id={"ey": to},
        )

    far_first = sorted(range(1, ny), key=lambda d: -min(d, ny - d))
    for c in range(CHUNKS):
        for d in far_first:
            basis_copy(d, c).start()
    own = pltpu.make_async_copy(
        basis.at[:, pl.ds(pl.multiple_of(ey * cells, 128), cells)],
        relaid.at[pl.ds(pl.multiple_of(ey * rows, rows), rows), :],
        own_sem,
    )
    own.start()

    turn = 1.0 / (2.0 * math.pi)
    s1, s2, s3 = split3(settings[...])
    lane = lax.broadcasted_iota(jnp.int32, (n_par, 128), 1)
    row = lax.broadcasted_iota(jnp.int32, (n_par, 128), 0)
    place = lax.rem(lane, n_par) == row
    slot = lane // n_par

    def spread_out(part, slots):
        hit = functools.reduce(jnp.logical_or, [slot == s for s in slots])
        select = jnp.where(place & hit, 1.0, 0.0).astype(jnp.bfloat16)
        return jnp.dot(part, select, preferred_element_type=jnp.float32)

    left = spread_out(s1, (0, 1, 4)) + spread_out(s2, (2, 3)) + spread_out(s3, (5,))
    left = left.astype(jnp.bfloat16)
    f1, f2, f3 = split3(frequencies[...] * turn)
    for s, part in enumerate((f1, f2, f1, f2, f3, f1)):
        freq_stack[s * n_par:(s + 1) * n_par, :] = part
    freq_stack[6 * n_par:, :] = jnp.zeros((128 - 6 * n_par, feat), jnp.bfloat16)
    scaling = math.sqrt(2.0 / feat)
    norm_acc[...] = jnp.zeros_like(norm_acc)

    def feature_step(t, carry):
        cols = pl.ds(pl.multiple_of(t * FEAT_TILE, FEAT_TILE), FEAT_TILE)
        u = jnp.dot(left, freq_stack[:, cols], preferred_element_type=jnp.float32)
        u = u + phases[:, cols] * turn
        r = u - jnp.floor(u + 0.5)
        w = r * r
        half = COS_POLY[4]
        for coef in COS_POLY[3::-1]:
            half = half * w + coef
        value = ((2.0 * scaling) * (half * half) - scaling).astype(jnp.bfloat16)
        phi[:, cols] = value
        wide = value.astype(jnp.float32)
        square = wide * wide
        total = square[:, :128]
        for j in range(128, FEAT_TILE, 128):
            total = total + square[:, j:j + 128]
        norm_acc[...] += total
        return carry

    lax.fori_loop(0, feat // FEAT_TILE, feature_step, 0)

    spread_acc[...] = jnp.zeros_like(spread_acc)

    def expert_step(i, carry):
        cov_copy(i).wait()
        projected = jnp.dot(phi[...], cov_buf[i], preferred_element_type=jnp.float32)
        square = projected * projected
        total = square[:, :128]
        for j in range(128, TILE, 128):
            total = total + square[:, j:j + 128]
        spread_acc[i // tiles] += total
        return carry

    lax.fori_loop(0, n_exp * tiles, expert_step, 0)

    for e in range(n_exp):
        post_copy(e).wait()
    means = jnp.dot(phi[...], post_buf[...], preferred_element_type=jnp.float32)
    prior = noise_var[...] + signal_scale[...] * jnp.sum(norm_acc[...], axis=1, keepdims=True)
    inverse = 1.0 / prior
    log_prior = jnp.log(prior)
    inv_prior[...] = inverse
    numerator = jnp.zeros((n_set, comp), jnp.float32)
    precision = jnp.zeros((n_set, comp), jnp.float32)
    for e in range(n_exp):
        spread = jnp.sum(spread_acc[e], axis=1, keepdims=True)
        variance = noise_var[...] + signal_scale[...] * spread
        robust = jnp.maximum(0.5 * (log_prior - jnp.log(variance)), 0.0)
        recip = 1.0 / variance
        numerator = numerator + robust * recip * means[:, e * comp:(e + 1) * comp]
        precision = precision + robust * (recip - inverse)
    parts[:, :comp] = numerator
    parts[:, comp:] = precision

    my_rows = pl.ds(pl.multiple_of(ex * block, block), block)

    def plane_copy(d):
        to = lax.rem(ex + d, nx)
        return pltpu.make_async_remote_copy(
            src_ref=parts.at[pl.ds(pl.multiple_of(to * block, block), block), :],
            dst_ref=plane_in.at[d - 1],
            send_sem=plane_send.at[d - 1],
            recv_sem=plane_recv.at[d - 1],
            device_id={"ex": to},
        )

    for d in range(1, nx):
        plane_copy(d).start()
    total = parts[my_rows, :]
    for d in range(1, nx):
        plane_copy(d).wait_recv()
        total = total + plane_in[d - 1]
    column_out[...] = total.astype(jnp.bfloat16)

    def column_copy(d):
        return pltpu.make_async_remote_copy(
            src_ref=column_out,
            dst_ref=column_in.at[d - 1],
            send_sem=column_send.at[d - 1],
            recv_sem=column_recv.at[d - 1],
            device_id={"ey": lax.rem(ey + d, ny)},
        )

    for d in far_first:
        column_copy(d).start()
    for d in range(1, ny):
        column_copy(d).wait_recv()
        total = total + column_in[d - 1].astype(jnp.float32)
    ratio = total[:, :comp] / (total[:, comp:] + inv_prior[my_rows, :])
    gathered[my_rows, :] = ratio.astype(jnp.bfloat16)

    def gather_copy(d, origin):
        at = pl.ds(pl.multiple_of(origin * block, block), block)
        return pltpu.make_async_remote_copy(
            src_ref=gathered.at[at, :],
            dst_ref=gathered.at[at, :],
            send_sem=gather_send.at[d - 1],
            recv_sem=gather_recv.at[d - 1],
            device_id={"ex": lax.rem(ex + d, nx)},
        )

    for d in range(1, nx):
        gather_copy(d, ex).start()
    for d in range(1, nx):
        gather_copy(d, lax.rem(ex + nx - d, nx)).wait_recv()
    for d in range(1, nx):
        gather_copy(d, ex).wait_send()
        plane_copy(d).wait_send()
    for d in range(1, ny):
        column_copy(d).wait_send()
    weights[...] = gathered[...]

    own.wait()
    for c in range(CHUNKS):
        for d in far_first:
            basis_copy(d, c).wait_send()
            basis_copy(d, c).wait_recv()


def field_kernel(weights, relaid, mean, out):
    stock = jnp.dot(weights[...], relaid[...], preferred_element_type=jnp.float32)
    out[...] = (stock + mean[...]).astype(out.dtype)


def per_device(
    nx, ny,
    settings, frequencies, phases, noise_var, signal_scale,
    cov_factor, post_mean, component_basis, mean_field,
):
    n_set = settings.shape[0]
    n_exp, feat, _ = cov_factor.shape
    comp = post_mean.shape[2]
    rows, wide_cells = component_basis.shape
    cells = wide_cells // ny
    block = n_set // nx
    n_tiles = n_exp * (feat // TILE)
    vmem = pl.BlockSpec(memory_space=pltpu.VMEM)
    hbm = pl.BlockSpec(memory_space=pl.ANY)
    dma = pltpu.SemaphoreType.DMA
    relaid, weights = pl.pallas_call(
        functools.partial(experts_kernel, nx, ny),
        out_shape=(
            jax.ShapeDtypeStruct((rows * ny, cells), jnp.bfloat16),
            jax.ShapeDtypeStruct((n_set, comp), jnp.bfloat16),
        ),
        in_specs=[vmem] * 5 + [hbm] * 3,
        out_specs=(hbm, vmem),
        scratch_shapes=[
            pltpu.VMEM((n_set, feat), jnp.bfloat16),
            pltpu.VMEM((128, feat), jnp.bfloat16),
            pltpu.VMEM((n_tiles, feat, TILE), jnp.bfloat16),
            pltpu.VMEM((feat, n_exp * comp), jnp.bfloat16),
            pltpu.VMEM((n_set, 128), jnp.float32),
            pltpu.VMEM((n_exp, n_set, 128), jnp.float32),
            pltpu.VMEM((n_set, comp), jnp.float32),
            pltpu.VMEM((n_set, 2 * comp), jnp.float32),
            pltpu.VMEM((nx - 1, block, 2 * comp), jnp.float32),
            pltpu.VMEM((block, 2 * comp), jnp.bfloat16),
            pltpu.VMEM((ny - 1, block, 2 * comp), jnp.bfloat16),
            pltpu.VMEM((n_set, comp), jnp.bfloat16),
            dma((n_tiles,)),
            dma((n_exp,)),
            dma,
            dma(((ny - 1) * CHUNKS,)),
            dma(((ny - 1) * CHUNKS,)),
            dma((nx - 1,)),
            dma((nx - 1,)),
            dma((ny - 1,)),
            dma((ny - 1,)),
            dma((nx - 1,)),
            dma((nx - 1,)),
        ],
        compiler_params=pltpu.CompilerParams(
            collective_id=0, has_side_effects=True, vmem_limit_bytes=48 * 1024 * 1024
        ),
        cost_estimate=pl.CostEstimate(
            flops=2 * n_set * feat * feat * n_exp,
            bytes_accessed=2 * n_exp * feat * feat + 4 * rows * wide_cells,
            transcendentals=n_set * feat,
        ),
        name="experts_and_exchange",
    )(
        settings, frequencies, phases[None, :], noise_var[None, :], signal_scale[None, :],
        cov_factor, post_mean, component_basis,
    )
    width = 1024
    return pl.pallas_call(
        field_kernel,
        out_shape=jax.ShapeDtypeStruct((n_set, cells), jnp.bfloat16),
        grid=(cells // width,),
        in_specs=[
            pl.BlockSpec((n_set, comp), lambda i: (0, 0)),
            pl.BlockSpec((rows * ny, width), lambda i: (0, i)),
            pl.BlockSpec((1, width), lambda i: (0, i)),
        ],
        out_specs=pl.BlockSpec((n_set, width), lambda i: (0, i)),
        compiler_params=pltpu.CompilerParams(vmem_limit_bytes=32 * 1024 * 1024),
        cost_estimate=pl.CostEstimate(
            flops=2 * n_set * comp * cells,
            bytes_accessed=2 * n_set * cells + 2 * comp * cells,
            transcendentals=0,
        ),
        name="carbon_field",
    )(weights, relaid, mean_field[None, :])


def solution(mesh):
    in_specs = (
        P(),
        P(),
        P(),
        P(),
        P(),
        P(("ex", "ey"), None, None),
        P(("ex", "ey"), None, None),
        P("ey", "ex"),
        P(("ex", "ey")),
    )
    out_specs = P(None, ("ex", "ey"))
    return jax.shard_map(
        functools.partial(per_device, mesh.shape["ex"], mesh.shape["ey"]),
        mesh=mesh, in_specs=in_specs, out_specs=out_specs, check_vma=False,
    )
```

```python
import functools
import math

import jax
import jax.numpy as jnp
from jax import lax
from jax.experimental import pallas as pl
from jax.experimental.pallas import tpu as pltpu
from jax.sharding import PartitionSpec as P

CHUNKS = 8
FIRST = 4
TILE = 512
FEAT_TILE = 256
COS_POLY = (0.9999999532, -4.9347928306, 4.0584113529, -1.3318765681, 0.2196896111)


def split3(x):
    first = x.astype(jnp.bfloat16)
    rest = x - first.astype(jnp.float32)
    second = rest.astype(jnp.bfloat16)
    third = (rest - second.astype(jnp.float32)).astype(jnp.bfloat16)
    return first, second, third


def experts_kernel(
    nx, ny,
    settings_hbm, frequencies_hbm, phases_hbm, noise_hbm, scale_hbm, cov, post, basis,
    relaid, weights,
    settings, frequencies, phases, noise_var, signal_scale, phi, freq_stack, cov_buf, post_buf, norm_acc, spread_acc, inv_prior,
    parts, plane_in, column_out, column_in, gathered,
    small_sem, cov_sem, post_sem, own_sem,
    basis_send, basis_recv, plane_send, plane_recv,
    column_send, column_recv, rows_send, rows_recv, gather_send, gather_recv,
):
    ex = lax.axis_index("ex")
    ey = lax.axis_index("ey")
    n_exp, feat, _ = cov.shape
    n_par, n_set = settings.shape
    comp = noise_var.shape[1]
    rows = basis.shape[0]
    cells = basis.shape[1] // ny
    chunk = cells // CHUNKS
    block = n_set // nx
    tiles = feat // TILE

    barrier = pltpu.get_barrier_semaphore()
    for d in range(1, ny):
        pl.semaphore_signal(barrier, inc=1, device_id={"ey": lax.rem(ey + d, ny)})
    for d in range(1, nx):
        pl.semaphore_signal(barrier, inc=1, device_id={"ex": lax.rem(ex + d, nx)})

    def cov_copy(i):
        e = i // tiles
        cols = pl.ds(pl.multiple_of((i % tiles) * TILE, TILE), TILE)
        return pltpu.make_async_copy(cov.at[e, :, cols], cov_buf.at[i], cov_sem.at[i])

    def post_copy(e):
        return pltpu.make_async_copy(
            post.at[e], post_buf.at[:, pl.ds(e * comp, comp)], post_sem.at[e]
        )

    pairs = (
        (settings_hbm, settings), (frequencies_hbm, frequencies), (phases_hbm, phases),
        (noise_hbm, noise_var), (scale_hbm, signal_scale),
    )
    small = [pltpu.make_async_copy(a, b, small_sem.at[i]) for i, (a, b) in enumerate(pairs)]
    for copy in small:
        copy.start()
    for i in range(n_exp * tiles):
        cov_copy(i).start()
    for e in range(n_exp):
        post_copy(e).start()

    pl.semaphore_wait(barrier, (nx - 1) + (ny - 1))

    def basis_copy(d, c):
        to = lax.rem(ey + d, ny)
        k = (d - 1) * CHUNKS + c
        return pltpu.make_async_remote_copy(
            src_ref=basis.at[:, pl.ds(pl.multiple_of(to * cells + c * chunk, 128), chunk)],
            dst_ref=relaid.at[pl.ds(pl.multiple_of(ey * rows, rows), rows), pl.ds(c * chunk, chunk)],
            send_sem=basis_send.at[k],
            recv_sem=basis_recv.at[k],
            device_id={"ey": to},
        )

    far_first = sorted(range(1, ny), key=lambda d: -min(d, ny - d))

    def send_chunks(lo, hi):
        for c in range(lo, hi):
            for d in far_first:
                basis_copy(d, c).start()

    send_chunks(0, FIRST)
    own = pltpu.make_async_copy(
        basis.at[:, pl.ds(pl.multiple_of(ey * cells, 128), cells)],
        relaid.at[pl.ds(pl.multiple_of(ey * rows, rows), rows), :],
        own_sem,
    )
    own.start()

    for copy in small:
        copy.wait()
    turn = 1.0 / (2.0 * math.pi)
    s1, s2, s3 = split3(settings[...])
    lane = lax.broadcasted_iota(jnp.int32, (n_par, 128), 1)
    row = lax.broadcasted_iota(jnp.int32, (n_par, 128), 0)
    place = lax.rem(lane, n_par) == row
    slot = lane // n_par

    def spread_out(part, slots):
        hit = functools.reduce(jnp.logical_or, [slot == s for s in slots])
        select = jnp.where(place & hit, 1.0, 0.0).astype(jnp.bfloat16)
        return lax.dot_general(
            part, select, (((0,), (0,)), ((), ())), preferred_element_type=jnp.float32
        )

    left = spread_out(s1, (0, 1, 4)) + spread_out(s2, (2, 3)) + spread_out(s3, (5,))
    left = left.astype(jnp.bfloat16)
    f1, f2, f3 = split3(frequencies[...] * turn)
    for s, part in enumerate((f1, f2, f1, f2, f3, f1)):
        freq_stack[s * n_par:(s + 1) * n_par, :] = part
    freq_stack[6 * n_par:, :] = jnp.zeros((128 - 6 * n_par, feat), jnp.bfloat16)
    scaling = math.sqrt(2.0 / feat)
    norm_acc[...] = jnp.zeros_like(norm_acc)

    def feature_step(t, carry):
        cols = pl.ds(pl.multiple_of(t * FEAT_TILE, FEAT_TILE), FEAT_TILE)
        u = jnp.dot(left, freq_stack[:, cols], preferred_element_type=jnp.float32)
        u = u + phases[:, cols] * turn
        r = u - jnp.floor(u + 0.5)
        w = r * r
        half = COS_POLY[4]
        for coef in COS_POLY[3::-1]:
            half = half * w + coef
        value = ((2.0 * scaling) * (half * half) - scaling).astype(jnp.bfloat16)
        phi[:, cols] = value
        wide = value.astype(jnp.float32)
        square = wide * wide
        total = square[:, :128]
        for j in range(128, FEAT_TILE, 128):
            total = total + square[:, j:j + 128]
        norm_acc[...] += total
        return carry

    lax.fori_loop(0, feat // FEAT_TILE, feature_step, 0)

    spread_acc[...] = jnp.zeros_like(spread_acc)

    def expert_step(i, carry):
        cov_copy(i).wait()
        projected = jnp.dot(phi[...], cov_buf[i], preferred_element_type=jnp.float32)
        square = projected * projected
        total = square[:, :128]
        for j in range(128, TILE, 128):
            total = total + square[:, j:j + 128]
        spread_acc[i // tiles] += total
        return carry

    lax.fori_loop(0, n_exp * tiles, expert_step, 0)

    for e in range(n_exp):
        post_copy(e).wait()
    means = jnp.dot(phi[...], post_buf[...], preferred_element_type=jnp.float32)
    prior = noise_var[...] + signal_scale[...] * jnp.sum(norm_acc[...], axis=1, keepdims=True)
    inverse = 1.0 / prior
    log_prior = jnp.log(prior)
    inv_prior[...] = inverse
    numerator = jnp.zeros((n_set, comp), jnp.float32)
    precision = jnp.zeros((n_set, comp), jnp.float32)
    for e in range(n_exp):
        spread = jnp.sum(spread_acc[e], axis=1, keepdims=True)
        variance = noise_var[...] + signal_scale[...] * spread
        robust = jnp.maximum(0.5 * (log_prior - jnp.log(variance)), 0.0)
        recip = 1.0 / variance
        numerator = numerator + robust * recip * means[:, e * comp:(e + 1) * comp]
        precision = precision + robust * (recip - inverse)
    parts[:, :comp] = numerator
    parts[:, comp:] = precision

    my_rows = pl.ds(pl.multiple_of(ex * block, block), block)

    def plane_copy(d):
        to = lax.rem(ex + d, nx)
        return pltpu.make_async_remote_copy(
            src_ref=parts.at[pl.ds(pl.multiple_of(to * block, block), block), :],
            dst_ref=plane_in.at[d - 1],
            send_sem=plane_send.at[d - 1],
            recv_sem=plane_recv.at[d - 1],
            device_id={"ex": to},
        )

    for d in range(1, nx):
        plane_copy(d).start()
    send_chunks(FIRST, FIRST + 1)
    total = parts[my_rows, :]
    for d in range(1, nx):
        plane_copy(d).wait_recv()
        total = total + plane_in[d - 1]
    column_out[...] = total

    share = block // ny if block % (16 * ny) == 0 else block
    thin = share == block

    def column_copy(d):
        to = lax.rem(ey + d, ny)
        first = 0 if thin else pl.multiple_of(to * share, share)
        return pltpu.make_async_remote_copy(
            src_ref=column_out.at[pl.ds(first, share), :],
            dst_ref=column_in.at[d - 1],
            send_sem=column_send.at[d - 1],
            recv_sem=column_recv.at[d - 1],
            device_id={"ey": to},
        )

    for d in far_first:
        column_copy(d).start()
    send_chunks(FIRST + 1, FIRST + 2)
    offset = 0 if thin else pl.multiple_of(ey * share, share)
    total = column_out[pl.ds(offset, share), :]
    for d in range(1, ny):
        column_copy(d).wait_recv()
        total = total + column_in[d - 1]
    share_rows = pl.ds(pl.multiple_of(ex * block + offset, share), share)
    ratio = total[:, :comp] / (total[:, comp:] + inv_prior[share_rows, :])
    gathered[share_rows, :] = ratio.astype(jnp.bfloat16)

    def rows_copy(d, origin):
        at = pl.ds(pl.multiple_of(ex * block + origin * share, share), share)
        return pltpu.make_async_remote_copy(
            src_ref=gathered.at[at, :],
            dst_ref=gathered.at[at, :],
            send_sem=rows_send.at[d - 1],
            recv_sem=rows_recv.at[d - 1],
            device_id={"ey": lax.rem(ey + d, ny)},
        )

    if not thin:
        for d in far_first:
            rows_copy(d, ey).start()
    send_chunks(FIRST + 2, FIRST + 3)
    if not thin:
        for d in range(1, ny):
            rows_copy(d, lax.rem(ey + ny - d, ny)).wait_recv()

    def gather_copy(d, origin):
        at = pl.ds(pl.multiple_of(origin * block, block), block)
        return pltpu.make_async_remote_copy(
            src_ref=gathered.at[at, :],
            dst_ref=gathered.at[at, :],
            send_sem=gather_send.at[d - 1],
            recv_sem=gather_recv.at[d - 1],
            device_id={"ex": lax.rem(ex + d, nx)},
        )

    for d in range(1, nx):
        gather_copy(d, ex).start()
    send_chunks(FIRST + 3, CHUNKS)
    for d in range(1, nx):
        gather_copy(d, lax.rem(ex + nx - d, nx)).wait_recv()
    for d in range(1, nx):
        gather_copy(d, ex).wait_send()
        plane_copy(d).wait_send()
    for d in range(1, ny):
        column_copy(d).wait_send()
        if not thin:
            rows_copy(d, ey).wait_send()
    weights[...] = gathered[...]

    own.wait()
    for c in range(CHUNKS):
        for d in far_first:
            basis_copy(d, c).wait_send()
            basis_copy(d, c).wait_recv()


def field_kernel(weights, relaid, mean, out):
    stock = jnp.dot(weights[...], relaid[...], preferred_element_type=jnp.float32)
    out[...] = (stock + mean[...]).astype(out.dtype)


def per_device(
    nx, ny,
    settings, frequencies, phases, noise_var, signal_scale,
    cov_factor, post_mean, component_basis, mean_field,
):
    n_set = settings.shape[0]
    n_exp, feat, _ = cov_factor.shape
    comp = post_mean.shape[2]
    rows, wide_cells = component_basis.shape
    cells = wide_cells // ny
    block = n_set // nx
    share = block // ny if block % (16 * ny) == 0 else block
    n_tiles = n_exp * (feat // TILE)
    vmem = pl.BlockSpec(memory_space=pltpu.VMEM)
    hbm = pl.BlockSpec(memory_space=pl.ANY)
    dma = pltpu.SemaphoreType.DMA
    relaid, weights = pl.pallas_call(
        functools.partial(experts_kernel, nx, ny),
        out_shape=(
            jax.ShapeDtypeStruct((rows * ny, cells), jnp.bfloat16),
            jax.ShapeDtypeStruct((n_set, comp), jnp.bfloat16),
        ),
        in_specs=[hbm] * 8,
        out_specs=(hbm, vmem),
        scratch_shapes=[
            pltpu.VMEM(settings.shape[::-1], jnp.float32),
            pltpu.VMEM(frequencies.shape, jnp.float32),
            pltpu.VMEM((1, feat), jnp.float32),
            pltpu.VMEM((1, comp), jnp.float32),
            pltpu.VMEM((1, comp), jnp.float32),
            pltpu.VMEM((n_set, feat), jnp.bfloat16),
            pltpu.VMEM((128, feat), jnp.bfloat16),
            pltpu.VMEM((n_tiles, feat, TILE), jnp.bfloat16),
            pltpu.VMEM((feat, n_exp * comp), jnp.bfloat16),
            pltpu.VMEM((n_set, 128), jnp.float32),
            pltpu.VMEM((n_exp, n_set, 128), jnp.float32),
            pltpu.VMEM((n_set, comp), jnp.float32),
            pltpu.VMEM((n_set, 2 * comp), jnp.float32),
            pltpu.VMEM((nx - 1, block, 2 * comp), jnp.float32),
            pltpu.VMEM((block, 2 * comp), jnp.float32),
            pltpu.VMEM((ny - 1, share, 2 * comp), jnp.float32),
            pltpu.VMEM((n_set, comp), jnp.bfloat16),
            dma((5,)),
            dma((n_tiles,)),
            dma((n_exp,)),
            dma,
            dma(((ny - 1) * CHUNKS,)),
            dma(((ny - 1) * CHUNKS,)),
            dma((nx - 1,)),
            dma((nx - 1,)),
            dma((ny - 1,)),
            dma((ny - 1,)),
            dma((ny - 1,)),
            dma((ny - 1,)),
            dma((nx - 1,)),
            dma((nx - 1,)),
        ],
        compiler_params=pltpu.CompilerParams(
            collective_id=0, has_side_effects=True, vmem_limit_bytes=60 * 1024 * 1024
        ),
        cost_estimate=pl.CostEstimate(
            flops=2 * n_set * feat * feat * n_exp,
            bytes_accessed=2 * n_exp * feat * feat + 4 * rows * wide_cells,
            transcendentals=n_set * feat,
        ),
        name="experts_and_exchange",
    )(
        settings.T, frequencies, phases[None, :], noise_var[None, :], signal_scale[None, :],
        cov_factor, post_mean, component_basis,
    )
    width = 1024
    return pl.pallas_call(
        field_kernel,
        out_shape=jax.ShapeDtypeStruct((n_set, cells), jnp.bfloat16),
        grid=(cells // width,),
        in_specs=[
            pl.BlockSpec((n_set, comp), lambda i: (0, 0)),
            pl.BlockSpec((rows * ny, width), lambda i: (0, i)),
            pl.BlockSpec((1, width), lambda i: (0, i)),
        ],
        out_specs=pl.BlockSpec((n_set, width), lambda i: (0, i)),
        compiler_params=pltpu.CompilerParams(vmem_limit_bytes=60 * 1024 * 1024),
        cost_estimate=pl.CostEstimate(
            flops=2 * n_set * comp * cells,
            bytes_accessed=2 * n_set * cells + 2 * comp * cells,
            transcendentals=0,
        ),
        name="carbon_field",
    )(weights, relaid, mean_field[None, :])


def solution(mesh):
    in_specs = (
        P(),
        P(),
        P(),
        P(),
        P(),
        P(("ex", "ey"), None, None),
        P(("ex", "ey"), None, None),
        P("ey", "ex"),
        P(("ex", "ey")),
    )
    out_specs = P(None, ("ex", "ey"))
    return jax.shard_map(
        functools.partial(per_device, mesh.shape["ex"], mesh.shape["ey"]),
        mesh=mesh, in_specs=in_specs, out_specs=out_specs, check_vma=False,
    )
```

```python
import functools
import math

import jax
import jax.numpy as jnp
from jax import lax
from jax.experimental import pallas as pl
from jax.experimental.pallas import tpu as pltpu
from jax.sharding import PartitionSpec as P

CHUNKS = 8
FIRST = 4
TILE = 512
FEAT_TILE = 256
COS_POLY = (0.9999999532, -4.9347928306, 4.0584113529, -1.3318765681, 0.2196896111)


def split3(x):
    first = x.astype(jnp.bfloat16)
    rest = x - first.astype(jnp.float32)
    second = rest.astype(jnp.bfloat16)
    third = (rest - second.astype(jnp.float32)).astype(jnp.bfloat16)
    return first, second, third


def experts_kernel(
    nx, ny,
    settings_hbm, frequencies_hbm, phases_hbm, noise_hbm, scale_hbm, cov, post, basis, mean_hbm,
    stock,
    settings, frequencies, phases, noise_var, signal_scale, mean, relaid, phi, freq_stack, cov_buf, post_buf, norm_acc, spread_acc, inv_prior,
    parts, plane_in, column_out, column_in, gathered,
    small_sem, cov_sem, post_sem, own_sem,
    basis_send, basis_recv, plane_send, plane_recv,
    column_send, column_recv, rows_send, rows_recv, gather_send, gather_recv,
):
    ex = lax.axis_index("ex")
    ey = lax.axis_index("ey")
    n_exp, feat, _ = cov.shape
    n_par, n_set = settings.shape
    comp = noise_var.shape[1]
    rows = basis.shape[0]
    cells = basis.shape[1] // ny
    chunk = cells // CHUNKS
    block = n_set // nx
    tiles = feat // TILE

    barrier = pltpu.get_barrier_semaphore()
    for d in range(1, ny):
        pl.semaphore_signal(barrier, inc=1, device_id={"ey": lax.rem(ey + d, ny)})
    for d in range(1, nx):
        pl.semaphore_signal(barrier, inc=1, device_id={"ex": lax.rem(ex + d, nx)})

    def cov_copy(i):
        e = i // tiles
        cols = pl.ds(pl.multiple_of((i % tiles) * TILE, TILE), TILE)
        return pltpu.make_async_copy(cov.at[e, :, cols], cov_buf.at[i], cov_sem.at[i])

    def post_copy(e):
        return pltpu.make_async_copy(
            post.at[e], post_buf.at[:, pl.ds(e * comp, comp)], post_sem.at[e]
        )

    pairs = (
        (settings_hbm, settings), (frequencies_hbm, frequencies), (phases_hbm, phases),
        (noise_hbm, noise_var), (scale_hbm, signal_scale), (mean_hbm, mean),
    )
    small = [pltpu.make_async_copy(a, b, small_sem.at[i]) for i, (a, b) in enumerate(pairs)]
    for copy in small:
        copy.start()
    for i in range(n_exp * tiles):
        cov_copy(i).start()
    for e in range(n_exp):
        post_copy(e).start()

    pl.semaphore_wait(barrier, (nx - 1) + (ny - 1))

    def basis_move(d, c, to, origin):
        k = (d - 1) * CHUNKS + c
        cols = pl.ds(pl.multiple_of(c * chunk, chunk), chunk)
        return pltpu.make_async_remote_copy(
            src_ref=basis.at[:, pl.ds(pl.multiple_of(to * cells + c * chunk, chunk), chunk)],
            dst_ref=relaid.at[pl.ds(pl.multiple_of(origin * rows, rows), rows), cols],
            send_sem=basis_send.at[k],
            recv_sem=basis_recv.at[k],
            device_id={"ey": to},
        )

    def basis_copy(d, c):
        return basis_move(d, c, lax.rem(ey + d, ny), ey)

    def basis_arrival(d, c):
        return basis_move(d, c, lax.rem(ey + d, ny), lax.rem(ey + ny - d, ny))

    far_first = sorted(range(1, ny), key=lambda d: -min(d, ny - d))

    def send_chunks(lo, hi):
        for c in range(lo, hi):
            for d in far_first:
                basis_copy(d, c).start()

    send_chunks(0, FIRST)
    own = pltpu.make_async_copy(
        basis.at[:, pl.ds(pl.multiple_of(ey * cells, 128), cells)],
        relaid.at[pl.ds(pl.multiple_of(ey * rows, rows), rows), :],
        own_sem,
    )
    own.start()

    for copy in small:
        copy.wait()
    turn = 1.0 / (2.0 * math.pi)
    s1, s2, s3 = split3(settings[...])
    lane = lax.broadcasted_iota(jnp.int32, (n_par, 128), 1)
    row = lax.broadcasted_iota(jnp.int32, (n_par, 128), 0)
    place = lax.rem(lane, n_par) == row
    slot = lane // n_par

    def spread_out(part, slots):
        hit = functools.reduce(jnp.logical_or, [slot == s for s in slots])
        select = jnp.where(place & hit, 1.0, 0.0).astype(jnp.bfloat16)
        return lax.dot_general(
            part, select, (((0,), (0,)), ((), ())), preferred_element_type=jnp.float32
        )

    left = spread_out(s1, (0, 1, 4)) + spread_out(s2, (2, 3)) + spread_out(s3, (5,))
    left = left.astype(jnp.bfloat16)
    f1, f2, f3 = split3(frequencies[...] * turn)
    for s, part in enumerate((f1, f2, f1, f2, f3, f1)):
        freq_stack[s * n_par:(s + 1) * n_par, :] = part
    freq_stack[6 * n_par:, :] = jnp.zeros((128 - 6 * n_par, feat), jnp.bfloat16)
    scaling = math.sqrt(2.0 / feat)
    norm_acc[...] = jnp.zeros_like(norm_acc)

    def feature_step(t, carry):
        cols = pl.ds(pl.multiple_of(t * FEAT_TILE, FEAT_TILE), FEAT_TILE)
        u = jnp.dot(left, freq_stack[:, cols], preferred_element_type=jnp.float32)
        u = u + phases[:, cols] * turn
        r = u - jnp.floor(u + 0.5)
        w = r * r
        half = COS_POLY[4]
        for coef in COS_POLY[3::-1]:
            half = half * w + coef
        value = ((2.0 * scaling) * (half * half) - scaling).astype(jnp.bfloat16)
        phi[:, cols] = value
        wide = value.astype(jnp.float32)
        square = wide * wide
        total = square[:, :128]
        for j in range(128, FEAT_TILE, 128):
            total = total + square[:, j:j + 128]
        norm_acc[...] += total
        return carry

    lax.fori_loop(0, feat // FEAT_TILE, feature_step, 0)

    spread_acc[...] = jnp.zeros_like(spread_acc)

    def expert_step(i, carry):
        cov_copy(i).wait()
        projected = jnp.dot(phi[...], cov_buf[i], preferred_element_type=jnp.float32)
        square = projected * projected
        total = square[:, :128]
        for j in range(128, TILE, 128):
            total = total + square[:, j:j + 128]
        spread_acc[i // tiles] += total
        return carry

    lax.fori_loop(0, n_exp * tiles, expert_step, 0)

    for e in range(n_exp):
        post_copy(e).wait()
    means = jnp.dot(phi[...], post_buf[...], preferred_element_type=jnp.float32)
    prior = noise_var[...] + signal_scale[...] * jnp.sum(norm_acc[...], axis=1, keepdims=True)
    inverse = 1.0 / prior
    log_prior = jnp.log(prior)
    inv_prior[...] = inverse
    numerator = jnp.zeros((n_set, comp), jnp.float32)
    precision = jnp.zeros((n_set, comp), jnp.float32)
    for e in range(n_exp):
        spread = jnp.sum(spread_acc[e], axis=1, keepdims=True)
        variance = noise_var[...] + signal_scale[...] * spread
        robust = jnp.maximum(0.5 * (log_prior - jnp.log(variance)), 0.0)
        recip = 1.0 / variance
        numerator = numerator + robust * recip * means[:, e * comp:(e + 1) * comp]
        precision = precision + robust * (recip - inverse)
    parts[:, :comp] = numerator
    parts[:, comp:] = precision

    my_rows = pl.ds(pl.multiple_of(ex * block, block), block)

    def plane_copy(d):
        to = lax.rem(ex + d, nx)
        return pltpu.make_async_remote_copy(
            src_ref=parts.at[pl.ds(pl.multiple_of(to * block, block), block), :],
            dst_ref=plane_in.at[d - 1],
            send_sem=plane_send.at[d - 1],
            recv_sem=plane_recv.at[d - 1],
            device_id={"ex": to},
        )

    for d in range(1, nx):
        plane_copy(d).start()
    send_chunks(FIRST, FIRST + 1)
    total = parts[my_rows, :]
    for d in range(1, nx):
        plane_copy(d).wait_recv()
        total = total + plane_in[d - 1]
    column_out[...] = total

    share = block // ny if block % (16 * ny) == 0 else block
    thin = share == block

    def column_copy(d):
        to = lax.rem(ey + d, ny)
        first = 0 if thin else pl.multiple_of(to * share, share)
        return pltpu.make_async_remote_copy(
            src_ref=column_out.at[pl.ds(first, share), :],
            dst_ref=column_in.at[d - 1],
            send_sem=column_send.at[d - 1],
            recv_sem=column_recv.at[d - 1],
            device_id={"ey": to},
        )

    for d in far_first:
        column_copy(d).start()
    send_chunks(FIRST + 1, FIRST + 2)
    offset = 0 if thin else pl.multiple_of(ey * share, share)
    total = column_out[pl.ds(offset, share), :]
    for d in range(1, ny):
        column_copy(d).wait_recv()
        total = total + column_in[d - 1]
    share_rows = pl.ds(pl.multiple_of(ex * block + offset, share), share)
    ratio = total[:, :comp] / (total[:, comp:] + inv_prior[share_rows, :])
    gathered[share_rows, :] = ratio.astype(jnp.bfloat16)

    def rows_copy(d, origin):
        at = pl.ds(pl.multiple_of(ex * block + origin * share, share), share)
        return pltpu.make_async_remote_copy(
            src_ref=gathered.at[at, :],
            dst_ref=gathered.at[at, :],
            send_sem=rows_send.at[d - 1],
            recv_sem=rows_recv.at[d - 1],
            device_id={"ey": lax.rem(ey + d, ny)},
        )

    if not thin:
        for d in far_first:
            rows_copy(d, ey).start()
    send_chunks(FIRST + 2, FIRST + 3)
    if not thin:
        for d in range(1, ny):
            rows_copy(d, lax.rem(ey + ny - d, ny)).wait_recv()

    def gather_copy(d, origin):
        at = pl.ds(pl.multiple_of(origin * block, block), block)
        return pltpu.make_async_remote_copy(
            src_ref=gathered.at[at, :],
            dst_ref=gathered.at[at, :],
            send_sem=gather_send.at[d - 1],
            recv_sem=gather_recv.at[d - 1],
            device_id={"ex": lax.rem(ex + d, nx)},
        )

    for d in range(1, nx):
        gather_copy(d, ex).start()
    send_chunks(FIRST + 3, CHUNKS)
    for d in range(1, nx):
        gather_copy(d, lax.rem(ex + nx - d, nx)).wait_recv()
    own.wait()

    def chunk_step(c, carry):
        for d in range(1, ny):
            basis_arrival(d, c).wait_recv()
        cols = pl.ds(pl.multiple_of(c * chunk, chunk), chunk)
        total = jnp.dot(gathered[...], relaid[:, cols], preferred_element_type=jnp.float32)
        stock[:, cols] = (total + mean[:, cols]).astype(stock.dtype)
        return carry

    lax.fori_loop(0, CHUNKS, chunk_step, 0)

    for d in range(1, nx):
        gather_copy(d, ex).wait_send()
        plane_copy(d).wait_send()
    for d in range(1, ny):
        column_copy(d).wait_send()
        if not thin:
            rows_copy(d, ey).wait_send()
        for c in range(CHUNKS):
            basis_copy(d, c).wait_send()


def per_device(
    nx, ny,
    settings, frequencies, phases, noise_var, signal_scale,
    cov_factor, post_mean, component_basis, mean_field,
):
    n_set = settings.shape[0]
    n_exp, feat, _ = cov_factor.shape
    comp = post_mean.shape[2]
    rows, wide_cells = component_basis.shape
    cells = wide_cells // ny
    block = n_set // nx
    share = block // ny if block % (16 * ny) == 0 else block
    n_tiles = n_exp * (feat // TILE)
    vmem = pl.BlockSpec(memory_space=pltpu.VMEM)
    hbm = pl.BlockSpec(memory_space=pltpu.HBM)
    dma = pltpu.SemaphoreType.DMA
    operands = (
        settings.T, frequencies, phases[None, :], noise_var[None, :], signal_scale[None, :],
        cov_factor, post_mean, component_basis, mean_field[None, :],
    )
    return pl.pallas_call(
        functools.partial(experts_kernel, nx, ny),
        out_shape=pltpu.VMEM((n_set, cells), jnp.bfloat16),
        in_specs=[hbm] * 9,
        out_specs=vmem,
        scratch_shapes=[
            pltpu.VMEM(settings.shape[::-1], jnp.float32),
            pltpu.VMEM(frequencies.shape, jnp.float32),
            pltpu.VMEM((1, feat), jnp.float32),
            pltpu.VMEM((1, comp), jnp.float32),
            pltpu.VMEM((1, comp), jnp.float32),
            pltpu.VMEM((1, cells), jnp.float32),
            pltpu.VMEM((rows * ny, cells), jnp.bfloat16),
            pltpu.VMEM((n_set, feat), jnp.bfloat16),
            pltpu.VMEM((128, feat), jnp.bfloat16),
            pltpu.VMEM((n_tiles, feat, TILE), jnp.bfloat16),
            pltpu.VMEM((feat, n_exp * comp), jnp.bfloat16),
            pltpu.VMEM((n_set, 128), jnp.float32),
            pltpu.VMEM((n_exp, n_set, 128), jnp.float32),
            pltpu.VMEM((n_set, comp), jnp.float32),
            pltpu.VMEM((n_set, 2 * comp), jnp.float32),
            pltpu.VMEM((nx - 1, block, 2 * comp), jnp.float32),
            pltpu.VMEM((block, 2 * comp), jnp.float32),
            pltpu.VMEM((ny - 1, share, 2 * comp), jnp.float32),
            pltpu.VMEM((n_set, comp), jnp.bfloat16),
            dma((6,)),
            dma((n_tiles,)),
            dma((n_exp,)),
            dma,
            dma(((ny - 1) * CHUNKS,)),
            dma(((ny - 1) * CHUNKS,)),
            dma((nx - 1,)),
            dma((nx - 1,)),
            dma((ny - 1,)),
            dma((ny - 1,)),
            dma((ny - 1,)),
            dma((ny - 1,)),
            dma((nx - 1,)),
            dma((nx - 1,)),
        ],
        compiler_params=pltpu.CompilerParams(
            collective_id=0, has_side_effects=True, vmem_limit_bytes=44 * 1024 * 1024
        ),
        cost_estimate=pl.CostEstimate(
            flops=2 * n_set * feat * feat * n_exp,
            bytes_accessed=2 * n_exp * feat * feat + 4 * rows * wide_cells,
            transcendentals=n_set * feat,
        ),
        name="experts_and_exchange",
    )(*(pltpu.with_memory_space_constraint(x, pltpu.HBM) for x in operands))


def solution(mesh):
    in_specs = (
        P(),
        P(),
        P(),
        P(),
        P(),
        P(("ex", "ey"), None, None),
        P(("ex", "ey"), None, None),
        P("ey", "ex"),
        P(("ex", "ey")),
    )
    out_specs = P(None, ("ex", "ey"))
    return jax.shard_map(
        functools.partial(per_device, mesh.shape["ex"], mesh.shape["ey"]),
        mesh=mesh, in_specs=in_specs, out_specs=out_specs, check_vma=False,
    )
```

```python
import functools
import math

import jax
import jax.numpy as jnp
from jax import lax
from jax.experimental import pallas as pl
from jax.experimental.pallas import tpu as pltpu
from jax.sharding import PartitionSpec as P

CHUNKS = 8
STAGES = (4.0, 5.67, 6.34, 7.0)
TILE = 512
FEAT_TILE = 256
COS_POLY = (0.9999999532, -4.9347928306, 4.0584113529, -1.3318765681, 0.2196896111)


def split3(x):
    first = x.astype(jnp.bfloat16)
    rest = x - first.astype(jnp.float32)
    second = rest.astype(jnp.bfloat16)
    third = (rest - second.astype(jnp.float32)).astype(jnp.bfloat16)
    return first, second, third


def experts_kernel(
    nx, ny,
    settings_hbm, frequencies_hbm, phases_hbm, noise_hbm, scale_hbm, cov, post, basis, mean_hbm,
    stock,
    settings, frequencies, phases, noise_var, signal_scale, mean, relaid, phi, freq_stack, cov_buf, post_buf, norm_acc, spread_acc, inv_prior,
    parts, plane_in, column_out, column_in, gathered,
    small_sem, cov_sem, post_sem, own_sem,
    basis_send, basis_recv, plane_send, plane_recv,
    column_send, column_recv, rows_send, rows_recv, gather_send, gather_recv,
):
    ex = lax.axis_index("ex")
    ey = lax.axis_index("ey")
    n_exp, feat, _ = cov.shape
    n_par, n_set = settings.shape
    comp = noise_var.shape[1]
    rows = basis.shape[0]
    cells = basis.shape[1] // ny
    chunk = cells // CHUNKS
    block = n_set // nx
    tiles = feat // TILE

    barrier = pltpu.get_barrier_semaphore()
    for d in range(1, ny):
        pl.semaphore_signal(barrier, inc=1, device_id={"ey": lax.rem(ey + d, ny)})
    for d in range(1, nx):
        pl.semaphore_signal(barrier, inc=1, device_id={"ex": lax.rem(ex + d, nx)})

    def cov_copy(i):
        e = i // tiles
        cols = pl.ds(pl.multiple_of((i % tiles) * TILE, TILE), TILE)
        return pltpu.make_async_copy(cov.at[e, :, cols], cov_buf.at[i], cov_sem.at[i])

    def post_copy(e):
        return pltpu.make_async_copy(
            post.at[e], post_buf.at[:, pl.ds(e * comp, comp)], post_sem.at[e]
        )

    pairs = (
        (settings_hbm, settings), (frequencies_hbm, frequencies), (phases_hbm, phases),
        (noise_hbm, noise_var), (scale_hbm, signal_scale), (mean_hbm, mean),
    )
    small = [pltpu.make_async_copy(a, b, small_sem.at[i]) for i, (a, b) in enumerate(pairs)]
    for copy in small:
        copy.start()
    for i in range(n_exp * tiles):
        cov_copy(i).start()
    for e in range(n_exp):
        post_copy(e).start()

    pl.semaphore_wait(barrier, (nx - 1) + (ny - 1))

    def basis_move(d, c, to, origin):
        k = (d - 1) * CHUNKS + c
        cols = pl.ds(pl.multiple_of(c * chunk, chunk), chunk)
        return pltpu.make_async_remote_copy(
            src_ref=basis.at[:, pl.ds(pl.multiple_of(to * cells + c * chunk, chunk), chunk)],
            dst_ref=relaid.at[pl.ds(pl.multiple_of(origin * rows, rows), rows), cols],
            send_sem=basis_send.at[k],
            recv_sem=basis_recv.at[k],
            device_id={"ey": to},
        )

    def basis_copy(d, c):
        return basis_move(d, c, lax.rem(ey + d, ny), ey)

    def basis_arrival(d, c):
        return basis_move(d, c, lax.rem(ey + d, ny), lax.rem(ey + ny - d, ny))

    far_first = sorted(range(1, ny), key=lambda d: -min(d, ny - d))

    order = [(d, c) for c in range(CHUNKS) for d in far_first]
    cuts = [0] + [round(s * len(order) / 8) for s in STAGES] + [len(order)]
    stages = [order[lo:hi] for lo, hi in zip(cuts, cuts[1:])]

    def send_mixed(stage, others):
        queue = list(stages[stage])
        for i, copy in enumerate(others):
            copy.start()
            while queue and len(stages[stage]) - len(queue) < (i + 1) * len(stages[stage]) // len(others):
                basis_copy(*queue.pop(0)).start()
        for pair in queue:
            basis_copy(*pair).start()

    send_mixed(0, [])
    own = pltpu.make_async_copy(
        basis.at[:, pl.ds(pl.multiple_of(ey * cells, 128), cells)],
        relaid.at[pl.ds(pl.multiple_of(ey * rows, rows), rows), :],
        own_sem,
    )
    own.start()

    for copy in small:
        copy.wait()
    turn = 1.0 / (2.0 * math.pi)
    s1, s2, s3 = split3(settings[...])
    lane = lax.broadcasted_iota(jnp.int32, (n_par, 128), 1)
    row = lax.broadcasted_iota(jnp.int32, (n_par, 128), 0)
    place = lax.rem(lane, n_par) == row
    slot = lane // n_par

    def spread_out(part, slots):
        hit = functools.reduce(jnp.logical_or, [slot == s for s in slots])
        select = jnp.where(place & hit, 1.0, 0.0).astype(jnp.bfloat16)
        return lax.dot_general(
            part, select, (((0,), (0,)), ((), ())), preferred_element_type=jnp.float32
        )

    left = spread_out(s1, (0, 1, 4)) + spread_out(s2, (2, 3)) + spread_out(s3, (5,))
    left = left.astype(jnp.bfloat16)
    f1, f2, f3 = split3(frequencies[...] * turn)
    for s, part in enumerate((f1, f2, f1, f2, f3, f1)):
        freq_stack[s * n_par:(s + 1) * n_par, :] = part
    freq_stack[6 * n_par:, :] = jnp.zeros((128 - 6 * n_par, feat), jnp.bfloat16)
    scaling = math.sqrt(2.0 / feat)
    norm_acc[...] = jnp.zeros_like(norm_acc)

    def feature_step(t, carry):
        cols = pl.ds(pl.multiple_of(t * FEAT_TILE, FEAT_TILE), FEAT_TILE)
        u = jnp.dot(left, freq_stack[:, cols], preferred_element_type=jnp.float32)
        u = u + phases[:, cols] * turn
        r = u - jnp.floor(u + 0.5)
        w = r * r
        half = COS_POLY[4]
        for coef in COS_POLY[3::-1]:
            half = half * w + coef
        value = ((2.0 * scaling) * (half * half) - scaling).astype(jnp.bfloat16)
        phi[:, cols] = value
        wide = value.astype(jnp.float32)
        square = wide * wide
        total = square[:, :128]
        for j in range(128, FEAT_TILE, 128):
            total = total + square[:, j:j + 128]
        norm_acc[...] += total
        return carry

    lax.fori_loop(0, feat // FEAT_TILE, feature_step, 0)

    spread_acc[...] = jnp.zeros_like(spread_acc)

    def expert_step(i, carry):
        cov_copy(i).wait()
        projected = jnp.dot(phi[...], cov_buf[i], preferred_element_type=jnp.float32)
        square = projected * projected
        total = square[:, :128]
        for j in range(128, TILE, 128):
            total = total + square[:, j:j + 128]
        spread_acc[i // tiles] += total
        return carry

    lax.fori_loop(0, n_exp * tiles, expert_step, 0)

    for e in range(n_exp):
        post_copy(e).wait()
    means = jnp.dot(phi[...], post_buf[...], preferred_element_type=jnp.float32)
    prior = noise_var[...] + signal_scale[...] * jnp.sum(norm_acc[...], axis=1, keepdims=True)
    inverse = 1.0 / prior
    log_prior = jnp.log(prior)
    inv_prior[...] = inverse
    numerator = jnp.zeros((n_set, comp), jnp.float32)
    precision = jnp.zeros((n_set, comp), jnp.float32)
    for e in range(n_exp):
        spread = jnp.sum(spread_acc[e], axis=1, keepdims=True)
        variance = noise_var[...] + signal_scale[...] * spread
        robust = jnp.maximum(0.5 * (log_prior - jnp.log(variance)), 0.0)
        recip = 1.0 / variance
        numerator = numerator + robust * recip * means[:, e * comp:(e + 1) * comp]
        precision = precision + robust * (recip - inverse)
    parts[:, :comp] = numerator
    parts[:, comp:] = precision

    my_rows = pl.ds(pl.multiple_of(ex * block, block), block)

    def plane_copy(d):
        to = lax.rem(ex + d, nx)
        return pltpu.make_async_remote_copy(
            src_ref=parts.at[pl.ds(pl.multiple_of(to * block, block), block), :],
            dst_ref=plane_in.at[d - 1],
            send_sem=plane_send.at[d - 1],
            recv_sem=plane_recv.at[d - 1],
            device_id={"ex": to},
        )

    send_mixed(1, [plane_copy(d) for d in range(1, nx)])
    total = parts[my_rows, :]
    for d in range(1, nx):
        plane_copy(d).wait_recv()
        total = total + plane_in[d - 1]
    column_out[...] = total

    share = block // ny if block % (16 * ny) == 0 else block
    thin = share == block

    def column_copy(d):
        to = lax.rem(ey + d, ny)
        first = 0 if thin else pl.multiple_of(to * share, share)
        return pltpu.make_async_remote_copy(
            src_ref=column_out.at[pl.ds(first, share), :],
            dst_ref=column_in.at[d - 1],
            send_sem=column_send.at[d - 1],
            recv_sem=column_recv.at[d - 1],
            device_id={"ey": to},
        )

    for d in far_first:
        column_copy(d).start()
    send_mixed(2, [])
    offset = 0 if thin else pl.multiple_of(ey * share, share)
    total = column_out[pl.ds(offset, share), :]
    for d in range(1, ny):
        column_copy(d).wait_recv()
        total = total + column_in[d - 1]
    share_rows = pl.ds(pl.multiple_of(ex * block + offset, share), share)
    ratio = total[:, :comp] / (total[:, comp:] + inv_prior[share_rows, :])
    gathered[share_rows, :] = ratio.astype(jnp.bfloat16)

    def rows_copy(d, origin):
        at = pl.ds(pl.multiple_of(ex * block + origin * share, share), share)
        return pltpu.make_async_remote_copy(
            src_ref=gathered.at[at, :],
            dst_ref=gathered.at[at, :],
            send_sem=rows_send.at[d - 1],
            recv_sem=rows_recv.at[d - 1],
            device_id={"ey": lax.rem(ey + d, ny)},
        )

    if not thin:
        for d in far_first:
            rows_copy(d, ey).start()
    send_mixed(3, [])
    if not thin:
        for d in range(1, ny):
            rows_copy(d, lax.rem(ey + ny - d, ny)).wait_recv()

    def gather_copy(d, origin):
        at = pl.ds(pl.multiple_of(origin * block, block), block)
        return pltpu.make_async_remote_copy(
            src_ref=gathered.at[at, :],
            dst_ref=gathered.at[at, :],
            send_sem=gather_send.at[d - 1],
            recv_sem=gather_recv.at[d - 1],
            device_id={"ex": lax.rem(ex + d, nx)},
        )

    send_mixed(4, [gather_copy(d, ex) for d in range(1, nx)])
    for d in range(1, nx):
        gather_copy(d, lax.rem(ex + nx - d, nx)).wait_recv()
    own.wait()

    def chunk_step(c, carry):
        for d in range(1, ny):
            basis_arrival(d, c).wait_recv()
        cols = pl.ds(pl.multiple_of(c * chunk, chunk), chunk)
        total = jnp.dot(gathered[...], relaid[:, cols], preferred_element_type=jnp.float32)
        stock[:, cols] = (total + mean[:, cols]).astype(stock.dtype)
        return carry

    lax.fori_loop(0, CHUNKS, chunk_step, 0)

    for d in range(1, nx):
        gather_copy(d, ex).wait_send()
        plane_copy(d).wait_send()
    for d in range(1, ny):
        column_copy(d).wait_send()
        if not thin:
            rows_copy(d, ey).wait_send()
        for c in range(CHUNKS):
            basis_copy(d, c).wait_send()


def per_device(
    nx, ny,
    settings, frequencies, phases, noise_var, signal_scale,
    cov_factor, post_mean, component_basis, mean_field,
):
    n_set = settings.shape[0]
    n_exp, feat, _ = cov_factor.shape
    comp = post_mean.shape[2]
    rows, wide_cells = component_basis.shape
    cells = wide_cells // ny
    block = n_set // nx
    share = block // ny if block % (16 * ny) == 0 else block
    n_tiles = n_exp * (feat // TILE)
    vmem = pl.BlockSpec(memory_space=pltpu.VMEM)
    hbm = pl.BlockSpec(memory_space=pltpu.HBM)
    dma = pltpu.SemaphoreType.DMA
    operands = (
        settings.T, frequencies, phases[None, :], noise_var[None, :], signal_scale[None, :],
        cov_factor, post_mean, component_basis, mean_field[None, :],
    )
    return pl.pallas_call(
        functools.partial(experts_kernel, nx, ny),
        out_shape=pltpu.VMEM((n_set, cells), jnp.bfloat16),
        in_specs=[hbm] * 9,
        out_specs=vmem,
        scratch_shapes=[
            pltpu.VMEM(settings.shape[::-1], jnp.float32),
            pltpu.VMEM(frequencies.shape, jnp.float32),
            pltpu.VMEM((1, feat), jnp.float32),
            pltpu.VMEM((1, comp), jnp.float32),
            pltpu.VMEM((1, comp), jnp.float32),
            pltpu.VMEM((1, cells), jnp.float32),
            pltpu.VMEM((rows * ny, cells), jnp.bfloat16),
            pltpu.VMEM((n_set, feat), jnp.bfloat16),
            pltpu.VMEM((128, feat), jnp.bfloat16),
            pltpu.VMEM((n_tiles, feat, TILE), jnp.bfloat16),
            pltpu.VMEM((feat, n_exp * comp), jnp.bfloat16),
            pltpu.VMEM((n_set, 128), jnp.float32),
            pltpu.VMEM((n_exp, n_set, 128), jnp.float32),
            pltpu.VMEM((n_set, comp), jnp.float32),
            pltpu.VMEM((n_set, 2 * comp), jnp.float32),
            pltpu.VMEM((nx - 1, block, 2 * comp), jnp.float32),
            pltpu.VMEM((block, 2 * comp), jnp.float32),
            pltpu.VMEM((ny - 1, share, 2 * comp), jnp.float32),
            pltpu.VMEM((n_set, comp), jnp.bfloat16),
            dma((6,)),
            dma((n_tiles,)),
            dma((n_exp,)),
            dma,
            dma(((ny - 1) * CHUNKS,)),
            dma(((ny - 1) * CHUNKS,)),
            dma((nx - 1,)),
            dma((nx - 1,)),
            dma((ny - 1,)),
            dma((ny - 1,)),
            dma((ny - 1,)),
            dma((ny - 1,)),
            dma((nx - 1,)),
            dma((nx - 1,)),
        ],
        compiler_params=pltpu.CompilerParams(
            collective_id=0, has_side_effects=True, vmem_limit_bytes=44 * 1024 * 1024
        ),
        cost_estimate=pl.CostEstimate(
            flops=2 * n_set * feat * feat * n_exp,
            bytes_accessed=2 * n_exp * feat * feat + 4 * rows * wide_cells,
            transcendentals=n_set * feat,
        ),
        name="experts_and_exchange",
    )(*(pltpu.with_memory_space_constraint(x, pltpu.HBM) for x in operands))


def solution(mesh):
    in_specs = (
        P(),
        P(),
        P(),
        P(),
        P(),
        P(("ex", "ey"), None, None),
        P(("ex", "ey"), None, None),
        P("ey", "ex"),
        P(("ex", "ey")),
    )
    out_specs = P(None, ("ex", "ey"))
    return jax.shard_map(
        functools.partial(per_device, mesh.shape["ex"], mesh.shape["ey"]),
        mesh=mesh, in_specs=in_specs, out_specs=out_specs, check_vma=False,
    )
```

```python
import functools
import math

import jax
import jax.numpy as jnp
from jax import lax
from jax.experimental import pallas as pl
from jax.experimental.pallas import tpu as pltpu
from jax.sharding import PartitionSpec as P

CHUNKS = 8
STAGES = (0.0, 3.0, 4.0, 4.67, 5.34, 8.0)
TILE = 512
FEAT_TILE = 256
COS_POLY = (0.9999999532, -4.9347928306, 4.0584113529, -1.3318765681, 0.2196896111)


def split3(x):
    first = x.astype(jnp.bfloat16)
    rest = x - first.astype(jnp.float32)
    second = rest.astype(jnp.bfloat16)
    third = (rest - second.astype(jnp.float32)).astype(jnp.bfloat16)
    return first, second, third


def experts_kernel(
    nx, ny,
    settings_hbm, frequencies_hbm, phases_hbm, noise_hbm, scale_hbm, cov, post, basis, mean_hbm,
    stock,
    settings, frequencies, phases, noise_var, signal_scale, mean, relaid, phi, freq_stack, cov_buf, post_buf, norm_acc, spread_acc, inv_prior,
    parts, plane_in, column_out, column_in, gathered,
    small_sem, cov_sem, post_sem, own_sem,
    basis_send, basis_recv, plane_send, plane_recv,
    column_send, column_recv, rows_send, rows_recv, gather_send, gather_recv,
):
    ex = lax.axis_index("ex")
    ey = lax.axis_index("ey")
    n_exp, feat, _ = cov.shape
    n_par, n_set = settings.shape
    comp = noise_var.shape[1]
    rows = basis.shape[0]
    cells = basis.shape[1] // ny
    chunk = cells // CHUNKS
    block = n_set // nx
    tiles = feat // TILE

    barrier = pltpu.get_barrier_semaphore()
    for d in range(1, ny):
        pl.semaphore_signal(barrier, inc=1, device_id={"ey": lax.rem(ey + d, ny)})
    for d in range(1, nx):
        pl.semaphore_signal(barrier, inc=1, device_id={"ex": lax.rem(ex + d, nx)})

    def cov_copy(i):
        e = i // tiles
        cols = pl.ds(pl.multiple_of((i % tiles) * TILE, TILE), TILE)
        return pltpu.make_async_copy(cov.at[e, :, cols], cov_buf.at[i], cov_sem.at[i])

    def post_copy(e):
        return pltpu.make_async_copy(
            post.at[e], post_buf.at[:, pl.ds(e * comp, comp)], post_sem.at[e]
        )

    pairs = (
        (settings_hbm, settings), (frequencies_hbm, frequencies), (phases_hbm, phases),
        (noise_hbm, noise_var), (scale_hbm, signal_scale), (mean_hbm, mean),
    )
    small = [pltpu.make_async_copy(a, b, small_sem.at[i]) for i, (a, b) in enumerate(pairs)]
    for copy in small:
        copy.start()
    for i in range(n_exp * tiles):
        cov_copy(i).start()
    for e in range(n_exp):
        post_copy(e).start()

    pl.semaphore_wait(barrier, (nx - 1) + (ny - 1))

    def basis_move(d, c, to, origin):
        k = (d - 1) * CHUNKS + c
        cols = pl.ds(pl.multiple_of(c * chunk, chunk), chunk)
        return pltpu.make_async_remote_copy(
            src_ref=basis.at[:, pl.ds(pl.multiple_of(to * cells + c * chunk, chunk), chunk)],
            dst_ref=relaid.at[pl.ds(pl.multiple_of(origin * rows, rows), rows), cols],
            send_sem=basis_send.at[k],
            recv_sem=basis_recv.at[k],
            device_id={"ey": to},
        )

    def basis_copy(d, c):
        return basis_move(d, c, lax.rem(ey + d, ny), ey)

    def basis_arrival(d, c):
        return basis_move(d, c, lax.rem(ey + d, ny), lax.rem(ey + ny - d, ny))

    far_first = sorted(range(1, ny), key=lambda d: -min(d, ny - d))

    order = [(d, c) for c in range(CHUNKS) for d in far_first]
    cuts = [round(s * len(order) / 8) for s in STAGES]

    def send_stage(stage):
        for d, c in order[cuts[stage]:cuts[stage + 1]]:
            basis_copy(d, c).start()

    send_stage(0)
    own = pltpu.make_async_copy(
        basis.at[:, pl.ds(pl.multiple_of(ey * cells, 128), cells)],
        relaid.at[pl.ds(pl.multiple_of(ey * rows, rows), rows), :],
        own_sem,
    )
    own.start()

    for copy in small:
        copy.wait()
    turn = 1.0 / (2.0 * math.pi)
    s1, s2, s3 = split3(settings[...])
    lane = lax.broadcasted_iota(jnp.int32, (n_par, 128), 1)
    row = lax.broadcasted_iota(jnp.int32, (n_par, 128), 0)
    place = lax.rem(lane, n_par) == row
    slot = lane // n_par

    def spread_out(part, slots):
        hit = functools.reduce(jnp.logical_or, [slot == s for s in slots])
        select = jnp.where(place & hit, 1.0, 0.0).astype(jnp.bfloat16)
        return lax.dot_general(
            part, select, (((0,), (0,)), ((), ())), preferred_element_type=jnp.float32
        )

    left = spread_out(s1, (0, 1, 4)) + spread_out(s2, (2, 3)) + spread_out(s3, (5,))
    left = left.astype(jnp.bfloat16)
    f1, f2, f3 = split3(frequencies[...] * turn)
    for s, part in enumerate((f1, f2, f1, f2, f3, f1)):
        freq_stack[s * n_par:(s + 1) * n_par, :] = part
    freq_stack[6 * n_par:, :] = jnp.zeros((128 - 6 * n_par, feat), jnp.bfloat16)
    scaling = math.sqrt(2.0 / feat)
    norm_acc[...] = jnp.zeros_like(norm_acc)

    def feature_step(t, carry):
        cols = pl.ds(pl.multiple_of(t * FEAT_TILE, FEAT_TILE), FEAT_TILE)
        u = jnp.dot(left, freq_stack[:, cols], preferred_element_type=jnp.float32)
        u = u + phases[:, cols] * turn
        r = u - jnp.floor(u + 0.5)
        w = r * r
        half = COS_POLY[4]
        for coef in COS_POLY[3::-1]:
            half = half * w + coef
        value = ((2.0 * scaling) * (half * half) - scaling).astype(jnp.bfloat16)
        phi[:, cols] = value
        wide = value.astype(jnp.float32)
        square = wide * wide
        total = square[:, :128]
        for j in range(128, FEAT_TILE, 128):
            total = total + square[:, j:j + 128]
        norm_acc[...] += total
        return carry

    lax.fori_loop(0, feat // FEAT_TILE, feature_step, 0)

    spread_acc[...] = jnp.zeros_like(spread_acc)

    def expert_step(i, carry):
        cov_copy(i).wait()
        projected = jnp.dot(phi[...], cov_buf[i], preferred_element_type=jnp.float32)
        square = projected * projected
        total = square[:, :128]
        for j in range(128, TILE, 128):
            total = total + square[:, j:j + 128]
        spread_acc[i // tiles] += total
        return carry

    lax.fori_loop(0, n_exp * tiles, expert_step, 0)

    for e in range(n_exp):
        post_copy(e).wait()
    means = jnp.dot(phi[...], post_buf[...], preferred_element_type=jnp.float32)
    prior = noise_var[...] + signal_scale[...] * jnp.sum(norm_acc[...], axis=1, keepdims=True)
    inverse = 1.0 / prior
    log_prior = jnp.log(prior)
    inv_prior[...] = inverse
    numerator = jnp.zeros((n_set, comp), jnp.float32)
    precision = jnp.zeros((n_set, comp), jnp.float32)
    for e in range(n_exp):
        spread = jnp.sum(spread_acc[e], axis=1, keepdims=True)
        variance = noise_var[...] + signal_scale[...] * spread
        robust = jnp.maximum(0.5 * (log_prior - jnp.log(variance)), 0.0)
        recip = 1.0 / variance
        numerator = numerator + robust * recip * means[:, e * comp:(e + 1) * comp]
        precision = precision + robust * (recip - inverse)
    parts[:, :comp] = numerator
    parts[:, comp:] = precision

    my_rows = pl.ds(pl.multiple_of(ex * block, block), block)

    def plane_copy(d):
        to = lax.rem(ex + d, nx)
        return pltpu.make_async_remote_copy(
            src_ref=parts.at[pl.ds(pl.multiple_of(to * block, block), block), :],
            dst_ref=plane_in.at[d - 1],
            send_sem=plane_send.at[d - 1],
            recv_sem=plane_recv.at[d - 1],
            device_id={"ex": to},
        )

    for d in range(1, nx):
        plane_copy(d).start()
    send_stage(1)
    total = parts[my_rows, :]
    for d in range(1, nx):
        plane_copy(d).wait_recv()
        total = total + plane_in[d - 1]
    column_out[...] = total

    share = block // ny if block % (16 * ny) == 0 else block
    thin = share == block

    def column_copy(d):
        to = lax.rem(ey + d, ny)
        first = 0 if thin else pl.multiple_of(to * share, share)
        return pltpu.make_async_remote_copy(
            src_ref=column_out.at[pl.ds(first, share), :],
            dst_ref=column_in.at[d - 1],
            send_sem=column_send.at[d - 1],
            recv_sem=column_recv.at[d - 1],
            device_id={"ey": to},
        )

    for d in far_first:
        column_copy(d).start()
    send_stage(2)
    offset = 0 if thin else pl.multiple_of(ey * share, share)
    total = column_out[pl.ds(offset, share), :]
    for d in range(1, ny):
        column_copy(d).wait_recv()
        total = total + column_in[d - 1]
    share_rows = pl.ds(pl.multiple_of(ex * block + offset, share), share)
    ratio = total[:, :comp] / (total[:, comp:] + inv_prior[share_rows, :])
    gathered[share_rows, :] = ratio.astype(jnp.bfloat16)

    def rows_copy(d, origin):
        at = pl.ds(pl.multiple_of(ex * block + origin * share, share), share)
        return pltpu.make_async_remote_copy(
            src_ref=gathered.at[at, :],
            dst_ref=gathered.at[at, :],
            send_sem=rows_send.at[d - 1],
            recv_sem=rows_recv.at[d - 1],
            device_id={"ey": lax.rem(ey + d, ny)},
        )

    if not thin:
        for d in far_first:
            rows_copy(d, ey).start()
    send_stage(3)
    if not thin:
        for d in range(1, ny):
            rows_copy(d, lax.rem(ey + ny - d, ny)).wait_recv()

    def gather_copy(d, origin):
        at = pl.ds(pl.multiple_of(origin * block, block), block)
        return pltpu.make_async_remote_copy(
            src_ref=gathered.at[at, :],
            dst_ref=gathered.at[at, :],
            send_sem=gather_send.at[d - 1],
            recv_sem=gather_recv.at[d - 1],
            device_id={"ex": lax.rem(ex + d, nx)},
        )

    for d in range(1, nx):
        gather_copy(d, ex).start()
    send_stage(4)
    for d in range(1, nx):
        gather_copy(d, lax.rem(ex + nx - d, nx)).wait_recv()
    own.wait()

    def chunk_step(c, carry):
        for d in range(1, ny):
            basis_arrival(d, c).wait_recv()
        cols = pl.ds(pl.multiple_of(c * chunk, chunk), chunk)
        total = jnp.dot(gathered[...], relaid[:, cols], preferred_element_type=jnp.float32)
        stock[:, cols] = (total + mean[:, cols]).astype(stock.dtype)
        return carry

    lax.fori_loop(0, CHUNKS, chunk_step, 0)

    for d in range(1, nx):
        gather_copy(d, ex).wait_send()
        plane_copy(d).wait_send()
    for d in range(1, ny):
        column_copy(d).wait_send()
        if not thin:
            rows_copy(d, ey).wait_send()
        for c in range(CHUNKS):
            basis_copy(d, c).wait_send()


def per_device(
    nx, ny,
    settings, frequencies, phases, noise_var, signal_scale,
    cov_factor, post_mean, component_basis, mean_field,
):
    n_set = settings.shape[0]
    n_exp, feat, _ = cov_factor.shape
    comp = post_mean.shape[2]
    rows, wide_cells = component_basis.shape
    cells = wide_cells // ny
    block = n_set // nx
    share = block // ny if block % (16 * ny) == 0 else block
    n_tiles = n_exp * (feat // TILE)
    vmem = pl.BlockSpec(memory_space=pltpu.VMEM)
    hbm = pl.BlockSpec(memory_space=pltpu.HBM)
    dma = pltpu.SemaphoreType.DMA
    operands = (
        settings.T, frequencies, phases[None, :], noise_var[None, :], signal_scale[None, :],
        cov_factor, post_mean, component_basis, mean_field[None, :],
    )
    return pl.pallas_call(
        functools.partial(experts_kernel, nx, ny),
        out_shape=pltpu.VMEM((n_set, cells), jnp.bfloat16),
        in_specs=[hbm] * 9,
        out_specs=vmem,
        scratch_shapes=[
            pltpu.VMEM(settings.shape[::-1], jnp.float32),
            pltpu.VMEM(frequencies.shape, jnp.float32),
            pltpu.VMEM((1, feat), jnp.float32),
            pltpu.VMEM((1, comp), jnp.float32),
            pltpu.VMEM((1, comp), jnp.float32),
            pltpu.VMEM((1, cells), jnp.float32),
            pltpu.VMEM((rows * ny, cells), jnp.bfloat16),
            pltpu.VMEM((n_set, feat), jnp.bfloat16),
            pltpu.VMEM((128, feat), jnp.bfloat16),
            pltpu.VMEM((n_tiles, feat, TILE), jnp.bfloat16),
            pltpu.VMEM((feat, n_exp * comp), jnp.bfloat16),
            pltpu.VMEM((n_set, 128), jnp.float32),
            pltpu.VMEM((n_exp, n_set, 128), jnp.float32),
            pltpu.VMEM((n_set, comp), jnp.float32),
            pltpu.VMEM((n_set, 2 * comp), jnp.float32),
            pltpu.VMEM((nx - 1, block, 2 * comp), jnp.float32),
            pltpu.VMEM((block, 2 * comp), jnp.float32),
            pltpu.VMEM((ny - 1, share, 2 * comp), jnp.float32),
            pltpu.VMEM((n_set, comp), jnp.bfloat16),
            dma((6,)),
            dma((n_tiles,)),
            dma((n_exp,)),
            dma,
            dma(((ny - 1) * CHUNKS,)),
            dma(((ny - 1) * CHUNKS,)),
            dma((nx - 1,)),
            dma((nx - 1,)),
            dma((ny - 1,)),
            dma((ny - 1,)),
            dma((ny - 1,)),
            dma((ny - 1,)),
            dma((nx - 1,)),
            dma((nx - 1,)),
        ],
        compiler_params=pltpu.CompilerParams(
            collective_id=0, has_side_effects=True, vmem_limit_bytes=44 * 1024 * 1024
        ),
        cost_estimate=pl.CostEstimate(
            flops=2 * n_set * feat * feat * n_exp,
            bytes_accessed=2 * n_exp * feat * feat + 4 * rows * wide_cells,
            transcendentals=n_set * feat,
        ),
        name="experts_and_exchange",
    )(*(pltpu.with_memory_space_constraint(x, pltpu.HBM) for x in operands))


def solution(mesh):
    in_specs = (
        P(),
        P(),
        P(),
        P(),
        P(),
        P(("ex", "ey"), None, None),
        P(("ex", "ey"), None, None),
        P("ey", "ex"),
        P(("ex", "ey")),
    )
    out_specs = P(None, ("ex", "ey"))
    return jax.shard_map(
        functools.partial(per_device, mesh.shape["ex"], mesh.shape["ey"]),
        mesh=mesh, in_specs=in_specs, out_specs=out_specs, check_vma=False,
    )
```

```python
import functools
import math

import jax
import jax.numpy as jnp
from jax import lax
from jax.experimental import pallas as pl
from jax.experimental.pallas import tpu as pltpu
from jax.sharding import PartitionSpec as P

CHUNKS = 8
FIRST = 4
TILE = 512
FEAT_TILE = 256
COS_POLY = (0.9999999532, -4.9347928306, 4.0584113529, -1.3318765681, 0.2196896111)


def split3(x):
    first = x.astype(jnp.bfloat16)
    rest = x - first.astype(jnp.float32)
    second = rest.astype(jnp.bfloat16)
    third = (rest - second.astype(jnp.float32)).astype(jnp.bfloat16)
    return first, second, third


def experts_kernel(
    nx, ny,
    settings_hbm, frequencies_hbm, phases_hbm, noise_hbm, scale_hbm, cov, post, basis, mean_hbm,
    stock,
    settings, frequencies, phases, noise_var, signal_scale, mean, relaid, phi, freq_stack, cov_buf, post_buf, norm_acc, spread_acc, inv_prior,
    parts, plane_in, column_out, column_in, gathered,
    small_sem, cov_sem, post_sem, own_sem,
    basis_send, basis_recv, plane_send, plane_recv,
    column_send, column_recv, rows_send, rows_recv, gather_send, gather_recv,
):
    ex = lax.axis_index("ex")
    ey = lax.axis_index("ey")
    n_exp, feat, _ = cov.shape
    n_par, n_set = settings.shape
    comp = noise_var.shape[1]
    rows = basis.shape[0]
    cells = basis.shape[1] // ny
    chunk = cells // CHUNKS
    block = n_set // nx
    tiles = feat // TILE

    barrier = pltpu.get_barrier_semaphore()
    for d in range(1, ny):
        pl.semaphore_signal(barrier, inc=1, device_id={"ey": lax.rem(ey + d, ny)})
    for d in range(1, nx):
        pl.semaphore_signal(barrier, inc=1, device_id={"ex": lax.rem(ex + d, nx)})

    def cov_copy(i):
        e = i // tiles
        cols = pl.ds(pl.multiple_of((i % tiles) * TILE, TILE), TILE)
        return pltpu.make_async_copy(cov.at[e, :, cols], cov_buf.at[i], cov_sem.at[i])

    def post_copy(e):
        return pltpu.make_async_copy(
            post.at[e], post_buf.at[:, pl.ds(e * comp, comp)], post_sem.at[e]
        )

    pairs = (
        (settings_hbm, settings), (frequencies_hbm, frequencies), (phases_hbm, phases),
        (noise_hbm, noise_var), (scale_hbm, signal_scale), (mean_hbm, mean),
    )
    small = [pltpu.make_async_copy(a, b, small_sem.at[i]) for i, (a, b) in enumerate(pairs)]
    for copy in small:
        copy.start()
    early = n_exp * tiles // 2
    for i in range(early):
        cov_copy(i).start()

    pl.semaphore_wait(barrier, (nx - 1) + (ny - 1))

    def basis_move(d, c, to, origin):
        k = (d - 1) * CHUNKS + c
        cols = pl.ds(pl.multiple_of(c * chunk, chunk), chunk)
        return pltpu.make_async_remote_copy(
            src_ref=basis.at[:, pl.ds(pl.multiple_of(to * cells + c * chunk, chunk), chunk)],
            dst_ref=relaid.at[pl.ds(pl.multiple_of(origin * rows, rows), rows), cols],
            send_sem=basis_send.at[k],
            recv_sem=basis_recv.at[k],
            device_id={"ey": to},
        )

    def basis_copy(d, c):
        return basis_move(d, c, lax.rem(ey + d, ny), ey)

    def basis_arrival(d, c):
        return basis_move(d, c, lax.rem(ey + d, ny), lax.rem(ey + ny - d, ny))

    far_first = sorted(range(1, ny), key=lambda d: -min(d, ny - d))

    def send_chunks(lo, hi):
        for c in range(lo, hi):
            for d in far_first:
                basis_copy(d, c).start()

    send_chunks(0, 1)
    for i in range(early, n_exp * tiles):
        cov_copy(i).start()
    for e in range(n_exp):
        post_copy(e).start()
    send_chunks(1, FIRST)
    own = pltpu.make_async_copy(
        basis.at[:, pl.ds(pl.multiple_of(ey * cells, 128), cells)],
        relaid.at[pl.ds(pl.multiple_of(ey * rows, rows), rows), :],
        own_sem,
    )
    own.start()

    for copy in small:
        copy.wait()
    turn = 1.0 / (2.0 * math.pi)
    s1, s2, s3 = split3(settings[...])
    lane = lax.broadcasted_iota(jnp.int32, (n_par, 128), 1)
    row = lax.broadcasted_iota(jnp.int32, (n_par, 128), 0)
    place = lax.rem(lane, n_par) == row
    slot = lane // n_par

    def spread_out(part, slots):
        hit = functools.reduce(jnp.logical_or, [slot == s for s in slots])
        select = jnp.where(place & hit, 1.0, 0.0).astype(jnp.bfloat16)
        return lax.dot_general(
            part, select, (((0,), (0,)), ((), ())), preferred_element_type=jnp.float32
        )

    left = spread_out(s1, (0, 1, 4)) + spread_out(s2, (2, 3)) + spread_out(s3, (5,))
    left = left.astype(jnp.bfloat16)
    f1, f2, f3 = split3(frequencies[...] * turn)
    for s, part in enumerate((f1, f2, f1, f2, f3, f1)):
        freq_stack[s * n_par:(s + 1) * n_par, :] = part
    freq_stack[6 * n_par:, :] = jnp.zeros((128 - 6 * n_par, feat), jnp.bfloat16)
    scaling = math.sqrt(2.0 / feat)
    norm_acc[...] = jnp.zeros_like(norm_acc)

    def feature_step(t, carry):
        cols = pl.ds(pl.multiple_of(t * FEAT_TILE, FEAT_TILE), FEAT_TILE)
        u = jnp.dot(left, freq_stack[:, cols], preferred_element_type=jnp.float32)
        u = u + phases[:, cols] * turn
        r = u - jnp.floor(u + 0.5)
        w = r * r
        half = COS_POLY[4]
        for coef in COS_POLY[3::-1]:
            half = half * w + coef
        value = ((2.0 * scaling) * (half * half) - scaling).astype(jnp.bfloat16)
        phi[:, cols] = value
        wide = value.astype(jnp.float32)
        square = wide * wide
        total = square[:, :128]
        for j in range(128, FEAT_TILE, 128):
            total = total + square[:, j:j + 128]
        norm_acc[...] += total
        return carry

    lax.fori_loop(0, feat // FEAT_TILE, feature_step, 0)

    spread_acc[...] = jnp.zeros_like(spread_acc)

    def expert_step(i, carry):
        cov_copy(i).wait()
        projected = jnp.dot(phi[...], cov_buf[i], preferred_element_type=jnp.float32)
        square = projected * projected
        total = square[:, :128]
        for j in range(128, TILE, 128):
            total = total + square[:, j:j + 128]
        spread_acc[i // tiles] += total
        return carry

    lax.fori_loop(0, n_exp * tiles, expert_step, 0)

    for e in range(n_exp):
        post_copy(e).wait()
    means = jnp.dot(phi[...], post_buf[...], preferred_element_type=jnp.float32)
    prior = noise_var[...] + signal_scale[...] * jnp.sum(norm_acc[...], axis=1, keepdims=True)
    inverse = 1.0 / prior
    log_prior = jnp.log(prior)
    inv_prior[...] = inverse
    numerator = jnp.zeros((n_set, comp), jnp.float32)
    precision = jnp.zeros((n_set, comp), jnp.float32)
    for e in range(n_exp):
        spread = jnp.sum(spread_acc[e], axis=1, keepdims=True)
        variance = noise_var[...] + signal_scale[...] * spread
        robust = jnp.maximum(0.5 * (log_prior - jnp.log(variance)), 0.0)
        recip = 1.0 / variance
        numerator = numerator + robust * recip * means[:, e * comp:(e + 1) * comp]
        precision = precision + robust * (recip - inverse)
    parts[:, :comp] = numerator
    parts[:, comp:] = precision

    my_rows = pl.ds(pl.multiple_of(ex * block, block), block)

    def plane_copy(d):
        to = lax.rem(ex + d, nx)
        return pltpu.make_async_remote_copy(
            src_ref=parts.at[pl.ds(pl.multiple_of(to * block, block), block), :],
            dst_ref=plane_in.at[d - 1],
            send_sem=plane_send.at[d - 1],
            recv_sem=plane_recv.at[d - 1],
            device_id={"ex": to},
        )

    for d in range(1, nx):
        plane_copy(d).start()
    send_chunks(FIRST, FIRST + 1)
    total = parts[my_rows, :]
    for d in range(1, nx):
        plane_copy(d).wait_recv()
        total = total + plane_in[d - 1]
    column_out[...] = total

    share = block // ny if block % (16 * ny) == 0 else block
    thin = share == block

    def column_copy(d):
        to = lax.rem(ey + d, ny)
        first = 0 if thin else pl.multiple_of(to * share, share)
        return pltpu.make_async_remote_copy(
            src_ref=column_out.at[pl.ds(first, share), :],
            dst_ref=column_in.at[d - 1],
            send_sem=column_send.at[d - 1],
            recv_sem=column_recv.at[d - 1],
            device_id={"ey": to},
        )

    for d in far_first:
        column_copy(d).start()
    send_chunks(FIRST + 1, FIRST + 2)
    offset = 0 if thin else pl.multiple_of(ey * share, share)
    total = column_out[pl.ds(offset, share), :]
    for d in range(1, ny):
        column_copy(d).wait_recv()
        total = total + column_in[d - 1]
    share_rows = pl.ds(pl.multiple_of(ex * block + offset, share), share)
    ratio = total[:, :comp] / (total[:, comp:] + inv_prior[share_rows, :])
    gathered[share_rows, :] = ratio.astype(jnp.bfloat16)

    def rows_copy(d, origin):
        at = pl.ds(pl.multiple_of(ex * block + origin * share, share), share)
        return pltpu.make_async_remote_copy(
            src_ref=gathered.at[at, :],
            dst_ref=gathered.at[at, :],
            send_sem=rows_send.at[d - 1],
            recv_sem=rows_recv.at[d - 1],
            device_id={"ey": lax.rem(ey + d, ny)},
        )

    if not thin:
        for d in far_first:
            rows_copy(d, ey).start()
    send_chunks(FIRST + 2, FIRST + 3)
    if not thin:
        for d in range(1, ny):
            rows_copy(d, lax.rem(ey + ny - d, ny)).wait_recv()

    def gather_copy(d, origin):
        at = pl.ds(pl.multiple_of(origin * block, block), block)
        return pltpu.make_async_remote_copy(
            src_ref=gathered.at[at, :],
            dst_ref=gathered.at[at, :],
            send_sem=gather_send.at[d - 1],
            recv_sem=gather_recv.at[d - 1],
            device_id={"ex": lax.rem(ex + d, nx)},
        )

    for d in range(1, nx):
        gather_copy(d, ex).start()
    send_chunks(FIRST + 3, CHUNKS)
    for d in range(1, nx):
        gather_copy(d, lax.rem(ex + nx - d, nx)).wait_recv()
    own.wait()

    def chunk_step(c, carry):
        for d in range(1, ny):
            basis_arrival(d, c).wait_recv()
        cols = pl.ds(pl.multiple_of(c * chunk, chunk), chunk)
        total = jnp.dot(gathered[...], relaid[:, cols], preferred_element_type=jnp.float32)
        stock[:, cols] = (total + mean[:, cols]).astype(stock.dtype)
        return carry

    lax.fori_loop(0, CHUNKS, chunk_step, 0)

    for d in range(1, nx):
        gather_copy(d, ex).wait_send()
        plane_copy(d).wait_send()
    for d in range(1, ny):
        column_copy(d).wait_send()
        if not thin:
            rows_copy(d, ey).wait_send()
        for c in range(CHUNKS):
            basis_copy(d, c).wait_send()


def per_device(
    nx, ny,
    settings, frequencies, phases, noise_var, signal_scale,
    cov_factor, post_mean, component_basis, mean_field,
):
    n_set = settings.shape[0]
    n_exp, feat, _ = cov_factor.shape
    comp = post_mean.shape[2]
    rows, wide_cells = component_basis.shape
    cells = wide_cells // ny
    block = n_set // nx
    share = block // ny if block % (16 * ny) == 0 else block
    n_tiles = n_exp * (feat // TILE)
    vmem = pl.BlockSpec(memory_space=pltpu.VMEM)
    hbm = pl.BlockSpec(memory_space=pltpu.HBM)
    dma = pltpu.SemaphoreType.DMA
    operands = (
        settings.T, frequencies, phases[None, :], noise_var[None, :], signal_scale[None, :],
        cov_factor, post_mean, component_basis, mean_field[None, :],
    )
    return pl.pallas_call(
        functools.partial(experts_kernel, nx, ny),
        out_shape=pltpu.VMEM((n_set, cells), jnp.bfloat16),
        in_specs=[hbm] * 9,
        out_specs=vmem,
        scratch_shapes=[
            pltpu.VMEM(settings.shape[::-1], jnp.float32),
            pltpu.VMEM(frequencies.shape, jnp.float32),
            pltpu.VMEM((1, feat), jnp.float32),
            pltpu.VMEM((1, comp), jnp.float32),
            pltpu.VMEM((1, comp), jnp.float32),
            pltpu.VMEM((1, cells), jnp.float32),
            pltpu.VMEM((rows * ny, cells), jnp.bfloat16),
            pltpu.VMEM((n_set, feat), jnp.bfloat16),
            pltpu.VMEM((128, feat), jnp.bfloat16),
            pltpu.VMEM((n_tiles, feat, TILE), jnp.bfloat16),
            pltpu.VMEM((feat, n_exp * comp), jnp.bfloat16),
            pltpu.VMEM((n_set, 128), jnp.float32),
            pltpu.VMEM((n_exp, n_set, 128), jnp.float32),
            pltpu.VMEM((n_set, comp), jnp.float32),
            pltpu.VMEM((n_set, 2 * comp), jnp.float32),
            pltpu.VMEM((nx - 1, block, 2 * comp), jnp.float32),
            pltpu.VMEM((block, 2 * comp), jnp.float32),
            pltpu.VMEM((ny - 1, share, 2 * comp), jnp.float32),
            pltpu.VMEM((n_set, comp), jnp.bfloat16),
            dma((6,)),
            dma((n_tiles,)),
            dma((n_exp,)),
            dma,
            dma(((ny - 1) * CHUNKS,)),
            dma(((ny - 1) * CHUNKS,)),
            dma((nx - 1,)),
            dma((nx - 1,)),
            dma((ny - 1,)),
            dma((ny - 1,)),
            dma((ny - 1,)),
            dma((ny - 1,)),
            dma((nx - 1,)),
            dma((nx - 1,)),
        ],
        compiler_params=pltpu.CompilerParams(
            collective_id=0, has_side_effects=True, vmem_limit_bytes=44 * 1024 * 1024
        ),
        cost_estimate=pl.CostEstimate(
            flops=2 * n_set * feat * feat * n_exp,
            bytes_accessed=2 * n_exp * feat * feat + 4 * rows * wide_cells,
            transcendentals=n_set * feat,
        ),
        name="experts_and_exchange",
    )(*(pltpu.with_memory_space_constraint(x, pltpu.HBM) for x in operands))


def solution(mesh):
    in_specs = (
        P(),
        P(),
        P(),
        P(),
        P(),
        P(("ex", "ey"), None, None),
        P(("ex", "ey"), None, None),
        P("ey", "ex"),
        P(("ex", "ey")),
    )
    out_specs = P(None, ("ex", "ey"))
    return jax.shard_map(
        functools.partial(per_device, mesh.shape["ex"], mesh.shape["ey"]),
        mesh=mesh, in_specs=in_specs, out_specs=out_specs, check_vma=False,
    )
```
